32 devices in a mesh: dp: 16 (over z, y, core), tensor: 2 (over x).
Axes of the slice: x: 2, y: 2, z: 4, core: 2. Of those that a mesh axis runs over, the one named last changes fastest.
Arguments:
- latent_tokens: bfloat16 [512, 32, 1152], P('tensor', 'dp'), may hold values from -6 to 6
- cond: bfloat16 [32, 1152], P('dp'), may hold values from -6 to 6
- mod_weight: bfloat16 [1152, 6, 1152], P('dp', None, 'tensor'), may hold values from -0.1875 to 0.1875
- qkv_weight: bfloat16 [1152, 3, 1152], P('dp', None, 'tensor'), may hold values from -0.1875 to 0.1875
- out_weight: bfloat16 [1152, 1152], P('tensor', 'dp'), may hold values from -0.75 to 0.75
- fc1_weight: bfloat16 [1152, 4608], P('dp', 'tensor'), may hold values from -0.1875 to 0.1875
- fc2_weight: bfloat16 [4608, 1152], P('tensor', 'dp'), may hold values from -0.09375 to 0.09375
- grad_out: bfloat16 [512, 32, 1152], P('tensor', 'dp'), may hold values from -6 to 6
Outputs:
- block_output: bfloat16 [512, 32, 1152], P('tensor', 'dp')
- grad_x: float32 [512, 32, 1152], P('tensor', 'dp')
- grad_cond: float32 [32, 1152], P('dp')
- grad_mod_weight: float32 [1152, 6, 1152], P('dp', None, 'tensor')
- grad_qkv_weight: float32 [1152, 3, 1152], P('dp', None, 'tensor')
- grad_out_weight: float32 [1152, 1152], P('tensor', 'dp')
- grad_fc1_weight: float32 [1152, 4608], P('dp', 'tensor')
- grad_fc2_weight: float32 [4608, 1152], P('tensor', 'dp')
The draws below stay inside these ranges and needn't reach their ends.
All inputs are finite; a program needn't handle non-finite values.
Results may differ from the reference program's by a relative error of at most 0.022.
The reference program's roundings to bfloat16 on the way count: a program that leaves them out, or rounds other values in their place, can miss the bound.
Values may be sent and summed in bfloat16 or wider, within the bound.
A program may use at most 192 MiB of HBM per device.

```python
import jax
import jax.numpy as jnp
from jax import lax

D = 1152
HEAD_DIM = 72
FF = 4608
SEQ = 512
LATENTS = 32


def with_spikes(entries, key, source, target, shards_of, factor):
    owner, partner = [(jnp.arange(entries.shape[axis_at]) // (entries.shape[axis_at] // shards_of)).reshape([-1 if axis == axis_at else 1 for axis in range(entries.ndim)]) for axis_at in (source, target)]
    chosen = jax.random.permutation(key, shards_of)[partner]
    strong = (owner == chosen) | (owner == (partner + shards_of // 2) % shards_of)
    return jnp.where(strong, factor * entries, entries)


def steps_of(rng, dims, pieces, smallest, top_value):
    def one(axis_at, blocks):
        heights = jax.random.uniform(jax.random.fold_in(jax.random.fold_in(rng, 6), axis_at), (blocks,), jnp.float32, smallest / len(pieces), top_value / len(pieces))
        return jnp.repeat(jnp.exp(heights), dims[axis_at] // blocks).reshape((-1,) + (1,) * (len(dims) - axis_at - 1))

    gain = one(*pieces[0])
    for cut in pieces[1:]:
        gain = gain * one(*cut)
    return gain


def noise(rng, dims, deviation, reach, shards=(), kind=jnp.bfloat16):
    loudness = steps_of(rng, dims, shards, -0.22, 0.18) if shards else 1.0
    entries = jax.random.normal(rng, dims, jnp.float32) * deviation * loudness
    return jnp.minimum(jnp.maximum(entries, -reach), reach).astype(kind)


def bell_draw_with(key, extent, scale, most, pieces, heavy, kind=jnp.bfloat16):
    entries = scale * jax.random.normal(key, extent, jnp.float32)
    if pieces:
        entries = entries * steps_of(key, extent, pieces, -0.22, 0.18)
    return jnp.clip(with_spikes(entries, jax.random.fold_in(key, 3), *heavy), -most, most).astype(kind)


def setup_inputs(seed: int = 0) -> dict:
    key_of = jax.random.split(jax.random.key(seed), 9)
    latent_tokens = noise(key_of[0], (SEQ, LATENTS, D), 1.0, 6.0, ((0, 2), (1, 16)))
    cond = noise(key_of[1], (LATENTS, D), 1.0, 6.0, ((0, 16),))
    mod_weight = noise(key_of[2], (D, 6, D), D ** -0.5, 0.1875, ((0, 16), (2, 2)))
    qkv_weight = noise(key_of[3], (D, 3, D), D ** -0.5, 0.1875, ((0, 16), (2, 2)))
    out_weight = noise(key_of[4], (D, D), (D // 16) ** -0.5, 0.75, ((0, 2), (1, 16)))
    fc1_weight = noise(key_of[5], (D, FF), D ** -0.5, 0.1875, ((0, 16), (1, 2)))
    fc2_weight = noise(key_of[6], (FF, D), FF ** -0.5, 0.09375, ((0, 2), (1, 16)))
    grad_out = bell_draw_with(key_of[7], (SEQ, LATENTS, D), 1.0, 6.0, ((0, 2), (1, 16)), (1, 2, 16, 2.0))
    return dict(latent_tokens=latent_tokens, cond=cond, mod_weight=mod_weight, qkv_weight=qkv_weight, out_weight=out_weight, fc1_weight=fc1_weight, fc2_weight=fc2_weight, grad_out=grad_out)


eps_norm = 1e-06
exact_mode = lax.Precision.HIGHEST

@jax.custom_vjp
def low(v):
    return lax.optimization_barrier(v.astype(jnp.bfloat16)).astype(jnp.float32)

@jax.custom_vjp
def low_back(v):
    return v

def low_keep(v):
    return (low(v), None)

def low_pass(kept, grad):
    return (grad,)

def back_keep(v):
    return (v, None)

def back_low(kept, grad):
    return (low(grad),)
low.defvjp(low_keep, low_pass)
low_back.defvjp(back_keep, back_low)

def layer_norm(values):
    centred = values - lax.optimization_barrier(jnp.mean(values, axis=-1, keepdims=True))
    return centred * lax.rsqrt(lax.optimization_barrier(jnp.mean(centred * centred, axis=-1, keepdims=True)) + eps_norm)

def diffusion_transformer_block(block_inputs, condition_vector, modulation_weight, query_key_value_weight, output_projection_weight, first_dense_weight, second_dense_weight):
    seq_len, num_lat, model_dim = block_inputs.shape
    num_heads = model_dim // HEAD_DIM
    silu_cond = low(jax.nn.silu(condition_vector))
    modulation = low_back(jnp.einsum('bd,dke->bke', silu_cond, modulation_weight, precision=exact_mode))
    shift_one, scale_one, gate_one, shift_two, scale_two, gate_two = [modulation[None, :, member] for member in range(6)]
    normed = low(layer_norm(block_inputs) * (1.0 + scale_one) + shift_one)
    triple = low_back(low(jnp.einsum('sbd,dke->sbke', normed, query_key_value_weight, precision=exact_mode)))
    queries = triple[:, :, 0].reshape(seq_len, num_lat, num_heads, HEAD_DIM)
    key_vec = triple[:, :, 1].reshape(seq_len, num_lat, num_heads, HEAD_DIM)
    values = triple[:, :, 2].reshape(seq_len, num_lat, num_heads, HEAD_DIM)
    scores = low_back(jnp.einsum('qbhe,kbhe->bhqk', queries, key_vec, precision=exact_mode) * HEAD_DIM ** (-0.5))
    attn_probs = jax.nn.softmax(scores, axis=-1)
    attended = jnp.einsum('bhqk,kbhe->qbhe', low(attn_probs), values, precision=exact_mode)
    attended = low_back(low(attended)).reshape(seq_len, num_lat, model_dim)
    branch = low_back(jnp.einsum('sbd,de->sbe', attended, output_projection_weight, precision=exact_mode))
    middle = block_inputs + gate_one * branch
    normed_two = low(layer_norm(middle) * (1.0 + scale_two) + shift_two)
    hidden = low_back(jnp.einsum('sbd,df->sbf', normed_two, first_dense_weight, precision=exact_mode))
    active = low(jax.nn.gelu(hidden, approximate=True))
    mlp_branch = low_back(jnp.einsum('sbf,fd->sbd', active, second_dense_weight, precision=exact_mode))
    return middle + gate_two * mlp_branch

def reference(latent_tokens, cond, mod_weight, qkv_weight, out_weight, fc1_weight, fc2_weight, grad_out):
    weight_matrices = tuple((matrix.astype(jnp.float32) for matrix in (mod_weight, qkv_weight, out_weight, fc1_weight, fc2_weight)))
    groups = LATENTS // 8
    block_inputs = latent_tokens.astype(jnp.float32).reshape(SEQ, groups, 8, D).transpose(1, 0, 2, 3)
    conditions = cond.astype(jnp.float32).reshape(groups, 8, D)
    cotangent = grad_out.astype(jnp.float32).reshape(SEQ, groups, 8, D).transpose(1, 0, 2, 3)

    def step(totals, packed):
        input_group, condition_group, group_cot = packed
        block_result, backward_map = jax.vjp(diffusion_transformer_block, input_group, condition_group, *weight_matrices)
        grads = backward_map(group_cot)
        totals = tuple((total + grad for total, grad in zip(totals, grads[2:])))
        return (totals, (block_result, grads[0], grads[1]))
    start = tuple((jnp.zeros_like(matrix) for matrix in weight_matrices))
    totals, (outputs, grad_in, grad_cd) = lax.scan(step, start, (block_inputs, conditions, cotangent))
    out_block = outputs.transpose(1, 0, 2, 3).reshape(SEQ, LATENTS, D).astype(jnp.bfloat16)
    grad_input = grad_in.transpose(1, 0, 2, 3).reshape(SEQ, LATENTS, D)
    grad_condition = grad_cd.reshape(LATENTS, D)
    return (out_block, grad_input, grad_condition, totals[0], totals[1], totals[2], totals[3], totals[4])
```

```python
import jax
import jax.numpy as jnp
from jax import lax
from jax.sharding import PartitionSpec as P

HEAD_DIM = 72


eps_norm = 1e-06


def layer_norm(values):
    centred = values - jnp.mean(values, axis=-1, keepdims=True)
    recip = lax.rsqrt(jnp.mean(centred * centred, axis=-1, keepdims=True) + eps_norm)
    return (centred * recip, recip)


def norm_back(grad_norm, normed, recip):
    inner = grad_norm - jnp.mean(grad_norm, axis=-1, keepdims=True)
    return recip * (inner - normed * jnp.mean(grad_norm * normed, axis=-1, keepdims=True))


def attend_one(queries, key_rows, value_rows):
    scores = jnp.einsum(
        "qhe,khe->hqk", queries, key_rows, preferred_element_type=jnp.float32
    ) * HEAD_DIM ** (-0.5)
    peak = jnp.max(scores, axis=-1, keepdims=True)
    raised = jnp.exp(scores - peak)
    total = jnp.sum(raised, axis=-1, keepdims=True)
    attn_probs = (raised / total).astype(jnp.bfloat16)
    attended = jnp.einsum(
        "hqk,khe->qhe", attn_probs, value_rows, preferred_element_type=jnp.float32
    )
    return (attended.astype(jnp.bfloat16), peak + jnp.log(total))


def attend_back(queries, key_rows, value_rows, grad_att, log_total):
    scale = HEAD_DIM ** (-0.5)
    scores = (
        jnp.einsum("qhe,khe->hqk", queries, key_rows, preferred_element_type=jnp.float32) * scale
    )
    attn_probs = jnp.exp(scores - log_total)
    probs_low = attn_probs.astype(jnp.bfloat16)
    grad_probs = jnp.einsum(
        "qhe,khe->hqk", grad_att, value_rows, preferred_element_type=jnp.float32
    )
    centre = jnp.sum(attn_probs * grad_probs, axis=-1, keepdims=True)
    grad_scores = (attn_probs * (grad_probs - centre)).astype(jnp.bfloat16)
    grad_q = (
        jnp.einsum("hqk,khe->qhe", grad_scores, key_rows, preferred_element_type=jnp.float32)
        * scale
    )
    grad_k = (
        jnp.einsum("hqk,qhe->khe", grad_scores, queries, preferred_element_type=jnp.float32) * scale
    )
    grad_v = jnp.einsum("hqk,qhe->khe", probs_low, grad_att, preferred_element_type=jnp.float32)
    return jnp.stack([grad_q, grad_k, grad_v], axis=1).astype(jnp.bfloat16)


def spread(rows):
    size = lax.axis_size("tensor")
    if size == 2:
        other = lax.ppermute(rows, "tensor", [(0, 1), (1, 0)])
        return jnp.concatenate([rows, other], axis=0)
    return lax.all_gather(rows, "tensor", axis=0, tiled=True)


def shrink(terms):
    size = lax.axis_size("tensor")
    if size == 2:
        half = terms.shape[0] // 2
        other = lax.ppermute(terms[half:].astype(jnp.bfloat16), "tensor", [(0, 1), (1, 0)])
        return terms[:half].astype(jnp.float32) + other.astype(jnp.float32)
    return lax.psum_scatter(
        terms.astype(jnp.bfloat16), "tensor", scatter_dimension=0, tiled=True
    ).astype(jnp.float32)


def body(latent_tokens, cond, mod_weight, qkv_weight, out_weight, fc1_weight, fc2_weight, grad_out):
    (
        query_key_value_weight,
        output_projection_weight,
        first_dense_weight,
        second_dense_weight,
    ) = (
        lax.all_gather(qkv_weight, "dp", axis=0, tiled=True),
        lax.all_gather(out_weight, "dp", axis=1, tiled=True),
        lax.all_gather(fc1_weight, "dp", axis=0, tiled=True),
        lax.all_gather(fc2_weight, "dp", axis=1, tiled=True),
    )
    num_lat = latent_tokens.shape[1]
    local_dim = query_key_value_weight.shape[2]
    local_heads = local_dim // HEAD_DIM
    cond_f = cond.astype(jnp.float32)
    silu_cond = jax.nn.silu(cond_f).astype(jnp.bfloat16)
    silu_all = lax.all_gather(silu_cond, "dp", axis=0, tiled=True)
    mod_rows = mod_weight.shape[0]
    silu_rows = lax.dynamic_slice_in_dim(
        silu_all, lax.axis_index("dp") * mod_rows, mod_rows, axis=1
    )
    mod_part = lax.psum_scatter(
        jnp.einsum("bd,dke->bke", silu_rows, mod_weight, preferred_element_type=jnp.float32),
        "dp",
        scatter_dimension=0,
        tiled=True,
    )
    modulation = lax.all_gather(mod_part, "tensor", axis=2, tiled=True)
    shift_one, scale_one, gate_one, shift_two, scale_two, gate_two = [
        modulation[None, :, member] for member in range(6)
    ]
    block_inputs = latent_tokens.astype(jnp.float32)
    normed_one, recip_one = layer_norm(block_inputs)
    h_one = (normed_one * (1.0 + scale_one) + shift_one).astype(jnp.bfloat16)
    h_one_all = spread(h_one)
    seq_len = h_one_all.shape[0]
    triple = jnp.einsum(
        "sbd,dke->sbke", h_one_all, query_key_value_weight, preferred_element_type=jnp.float32
    ).astype(jnp.bfloat16)
    by_latent = jnp.moveaxis(triple, 1, 0).reshape(num_lat, seq_len, 3, local_heads, HEAD_DIM)
    q_lat = by_latent[:, :, 0]
    k_lat = by_latent[:, :, 1]
    v_lat = by_latent[:, :, 2]
    att_lat, log_total = jax.vmap(attend_one)(q_lat, k_lat, v_lat)
    attended = jnp.moveaxis(att_lat, 0, 1).reshape(seq_len, num_lat, local_dim)
    rows = attended
    branch = shrink(
        jnp.einsum(
            "sbh,hd->sbd", rows, output_projection_weight, preferred_element_type=jnp.float32
        )
    )
    middle = block_inputs + gate_one * branch
    normed_two, recip_two = layer_norm(middle)
    h_two = (normed_two * (1.0 + scale_two) + shift_two).astype(jnp.bfloat16)
    h_two_all = spread(h_two)
    hidden = jnp.einsum(
        "sbd,df->sbf", h_two_all, first_dense_weight, preferred_element_type=jnp.float32
    )
    active = jax.nn.gelu(hidden, approximate=True).astype(jnp.bfloat16)
    rows = active
    mlp_branch = shrink(
        jnp.einsum(
            "sbf,fd->sbd", rows, second_dense_weight, preferred_element_type=jnp.float32
        )
    )
    out_block = (middle + gate_two * mlp_branch).astype(jnp.bfloat16)
    cotangent = grad_out.astype(jnp.float32)
    grad_gate_two = jnp.sum(cotangent * mlp_branch, axis=0)
    grad_mlp = (cotangent * gate_two).astype(jnp.bfloat16)
    grad_mlp_all = spread(grad_mlp)
    grad_fc2 = jnp.einsum("sbf,sbd->fd", active, grad_mlp_all, preferred_element_type=jnp.float32)
    grad_active = jnp.einsum(
        "sbd,fd->sbf", grad_mlp_all, second_dense_weight, preferred_element_type=jnp.float32
    )
    gelu_value, gelu_pull = jax.vjp(lambda inner: jax.nn.gelu(inner, approximate=True), hidden)
    grad_hidden = gelu_pull(grad_active)[0].astype(jnp.bfloat16)
    grad_fc1 = jnp.einsum("sbd,sbf->df", h_two_all, grad_hidden, preferred_element_type=jnp.float32)
    mlp_grads = (grad_fc1, grad_fc2)
    rows = grad_hidden
    grad_h_two = shrink(
        jnp.einsum(
            "sbf,df->sbd", rows, first_dense_weight, preferred_element_type=jnp.float32
        )
    )
    grad_shift_two = jnp.sum(grad_h_two, axis=0)
    grad_scale_two = jnp.sum(grad_h_two * normed_two, axis=0)
    grad_middle = cotangent + norm_back(grad_h_two * (1.0 + scale_two), normed_two, recip_two)
    grad_gate_one = jnp.sum(grad_middle * branch, axis=0)
    grad_branch = (grad_middle * gate_one).astype(jnp.bfloat16)
    grad_branch_all = spread(grad_branch)
    grad_wout = jnp.einsum(
        "sbh,sbd->hd", attended, grad_branch_all, preferred_element_type=jnp.float32
    )
    grad_att = jnp.einsum(
        "sbd,hd->sbh", grad_branch_all, output_projection_weight, preferred_element_type=jnp.float32
    ).astype(jnp.bfloat16)
    grad_att_lat = jnp.moveaxis(grad_att, 1, 0).reshape(num_lat, seq_len, local_heads, HEAD_DIM)
    grad_triple_lat = jax.vmap(attend_back)(q_lat, k_lat, v_lat, grad_att_lat, log_total)
    grad_triple = jnp.moveaxis(grad_triple_lat, 0, 1).reshape(seq_len, num_lat, 3, local_dim)
    grad_wqkv = jnp.einsum(
        "sbd,sbke->dke", h_one_all, grad_triple, preferred_element_type=jnp.float32
    )
    rows = grad_triple
    grad_h_one = shrink(
        jnp.einsum(
            "sbke,dke->sbd", rows, query_key_value_weight, preferred_element_type=jnp.float32
        )
    )
    grad_shift_one = jnp.sum(grad_h_one, axis=0)
    grad_scale_one = jnp.sum(grad_h_one * normed_one, axis=0)
    grad_input = grad_middle + norm_back(grad_h_one * (1.0 + scale_one), normed_one, recip_one)
    grad_mod_part = jnp.stack(
        [
            grad_shift_one,
            grad_scale_one,
            grad_gate_one,
            grad_shift_two,
            grad_scale_two,
            grad_gate_two,
        ],
        axis=1,
    )
    grad_mod = lax.psum_scatter(
        grad_mod_part, "tensor", scatter_dimension=2, tiled=True
    ).astype(jnp.bfloat16)
    grad_mod_all = lax.all_gather(grad_mod, "dp", axis=0, tiled=True)
    grad_wmod = jnp.einsum(
        "bd,bke->dke", silu_rows, grad_mod_all, preferred_element_type=jnp.float32
    )
    grad_silu_part = jnp.einsum(
        "bke,dke->bd", grad_mod_all, mod_weight, preferred_element_type=jnp.float32
    )
    grad_silu_part = lax.all_to_all(grad_silu_part, "dp", split_axis=0, concat_axis=1, tiled=True)
    grad_silu = lax.psum(grad_silu_part, "tensor")
    silu_value, silu_pull = jax.vjp(jax.nn.silu, cond_f)
    grad_condition = silu_pull(grad_silu)[0]
    grad_b, grad_c, grad_d, grad_e = (
        lax.psum_scatter(
            grad_wqkv.astype(jnp.bfloat16), "dp", scatter_dimension=0, tiled=True
        ).astype(jnp.float32),
        lax.psum_scatter(
            grad_wout.astype(jnp.bfloat16), "dp", scatter_dimension=1, tiled=True
        ).astype(jnp.float32),
        lax.psum_scatter(
            mlp_grads[0].astype(jnp.bfloat16), "dp", scatter_dimension=0, tiled=True
        ).astype(jnp.float32),
        lax.psum_scatter(
            mlp_grads[1].astype(jnp.bfloat16), "dp", scatter_dimension=1, tiled=True
        ).astype(jnp.float32),
    )
    return (out_block, grad_input, grad_condition, grad_wmod, grad_b, grad_c, grad_d, grad_e)


def solution(mesh):
    return jax.shard_map(
        body,
        mesh=mesh,
        in_specs=(
            P("tensor", "dp", None),
            P("dp", None),
            P("dp", None, "tensor"),
            P("dp", None, "tensor"),
            P("tensor", "dp"),
            P("dp", "tensor"),
            P("tensor", "dp"),
            P("tensor", "dp", None),
        ),
        out_specs=(
            P("tensor", "dp", None),
            P("tensor", "dp", None),
            P("dp", None),
            P("dp", None, "tensor"),
            P("dp", None, "tensor"),
            P("tensor", "dp"),
            P("dp", "tensor"),
            P("tensor", "dp"),
        ),
        check_vma=False,
    )
```

```python
import jax
import jax.numpy as jnp
from jax import lax
from jax.sharding import PartitionSpec as P

HEAD_DIM = 72


eps_norm = 1e-06


def layer_norm(values):
    centred = values - jnp.mean(values, axis=-1, keepdims=True)
    recip = lax.rsqrt(jnp.mean(centred * centred, axis=-1, keepdims=True) + eps_norm)
    return (centred * recip, recip)


def norm_back(grad_norm, normed, recip):
    inner = grad_norm - jnp.mean(grad_norm, axis=-1, keepdims=True)
    return recip * (inner - normed * jnp.mean(grad_norm * normed, axis=-1, keepdims=True))


def attend_one(queries, key_rows, value_rows):
    scores = jnp.einsum(
        "qhe,khe->hqk", queries, key_rows, preferred_element_type=jnp.float32
    ) * HEAD_DIM ** (-0.5)
    peak = jnp.max(scores, axis=-1, keepdims=True)
    raised = jnp.exp(scores - peak)
    total = jnp.sum(raised, axis=-1, keepdims=True)
    attn_probs = (raised / total).astype(jnp.bfloat16)
    attended = jnp.einsum(
        "hqk,khe->qhe", attn_probs, value_rows, preferred_element_type=jnp.float32
    )
    return (attended.astype(jnp.bfloat16), peak + jnp.log(total))


def attend_back(queries, key_rows, value_rows, grad_att, log_total):
    scale = HEAD_DIM ** (-0.5)
    scores = (
        jnp.einsum("qhe,khe->hqk", queries, key_rows, preferred_element_type=jnp.float32) * scale
    )
    attn_probs = jnp.exp(scores - log_total)
    probs_low = attn_probs.astype(jnp.bfloat16)
    grad_probs = jnp.einsum(
        "qhe,khe->hqk", grad_att, value_rows, preferred_element_type=jnp.float32
    )
    centre = jnp.sum(attn_probs * grad_probs, axis=-1, keepdims=True)
    grad_scores = (attn_probs * (grad_probs - centre)).astype(jnp.bfloat16)
    grad_q = (
        jnp.einsum("hqk,khe->qhe", grad_scores, key_rows, preferred_element_type=jnp.float32)
        * scale
    )
    grad_k = (
        jnp.einsum("hqk,qhe->khe", grad_scores, queries, preferred_element_type=jnp.float32) * scale
    )
    grad_v = jnp.einsum("hqk,qhe->khe", probs_low, grad_att, preferred_element_type=jnp.float32)
    return jnp.stack([grad_q, grad_k, grad_v], axis=1).astype(jnp.bfloat16)


SWAP = [(0, 1), (1, 0)]


def paired():
    return lax.axis_size("tensor") == 2


def spread(rows):
    if paired():
        return jnp.concatenate([rows, lax.ppermute(rows, "tensor", SWAP)], axis=0)
    return lax.all_gather(rows, "tensor", axis=0, tiled=True)


def shrink(terms, beside=()):
    terms = terms.astype(jnp.bfloat16)
    if paired():
        half = terms.shape[0] // 2
        other = lax.ppermute(terms[half:], "tensor", SWAP)
        other, beside = lax.optimization_barrier((other, beside))
        return terms[:half].astype(jnp.float32) + other.astype(jnp.float32), beside
    total = lax.psum_scatter(terms, "tensor", scatter_dimension=0, tiled=True)
    return total.astype(jnp.float32), beside


def widen(part):
    if paired():
        other = lax.ppermute(part, "tensor", SWAP)
        first = lax.axis_index("tensor") == 0
        return jnp.where(
            first,
            jnp.concatenate([part, other], axis=-1),
            jnp.concatenate([other, part], axis=-1),
        )
    return lax.all_gather(part, "tensor", axis=2, tiled=True)


def narrow(terms):
    if paired():
        half = terms.shape[2] // 2
        first = lax.axis_index("tensor") == 0
        low, high = terms[:, :, :half], terms[:, :, half:]
        other = lax.ppermute(jnp.where(first, high, low), "tensor", SWAP)
        return jnp.where(first, low, high) + other
    return lax.psum_scatter(terms, "tensor", scatter_dimension=2, tiled=True)


def scatter_rows(grad):
    return lax.psum_scatter(grad, "dp", scatter_dimension=0, tiled=True).astype(jnp.float32)


def body(latent_tokens, cond, mod_weight, qkv_weight, out_weight, fc1_weight, fc2_weight, grad_out):
    num_lat = latent_tokens.shape[1]
    local_dim = qkv_weight.shape[2]
    mod_rows = mod_weight.shape[0]
    cond_f = cond.astype(jnp.float32)
    silu_cond = jax.nn.silu(cond_f).astype(jnp.bfloat16)
    silu_rows = lax.all_to_all(silu_cond, "dp", split_axis=1, concat_axis=0, tiled=True)
    mod_terms = jnp.einsum(
        "bd,dke->bke", silu_rows, mod_weight, preferred_element_type=jnp.float32
    )
    mod_terms = mod_terms.reshape(-1, num_lat, 6 * local_dim)
    mod_terms = lax.all_to_all(mod_terms, "dp", split_axis=0, concat_axis=0, tiled=True)
    mod_part = jnp.sum(mod_terms, axis=0).reshape(num_lat, 6, local_dim)
    modulation = widen(mod_part)
    attn_rows = jnp.concatenate([qkv_weight.reshape(mod_rows, -1), out_weight.T], axis=1)
    attn_weight = lax.all_gather(attn_rows, "dp", axis=0, tiled=True)
    first_dense_weight = lax.all_gather(fc1_weight, "dp", axis=0, tiled=True)
    second_dense_weight = lax.all_gather(fc2_weight.T, "dp", axis=0, tiled=True)
    query_key_value_weight = attn_weight[:, : 3 * local_dim]
    output_projection_weight = attn_weight[:, 3 * local_dim :]
    local_heads = local_dim // HEAD_DIM
    shift_one, scale_one, gate_one, shift_two, scale_two, gate_two = [
        modulation[None, :, member] for member in range(6)
    ]
    block_inputs = latent_tokens.astype(jnp.float32)
    normed_one, recip_one = layer_norm(block_inputs)
    h_one = (normed_one * (1.0 + scale_one) + shift_one).astype(jnp.bfloat16)
    h_one_all = spread(h_one)
    seq_len = h_one_all.shape[0]
    triple = jnp.einsum(
        "sbd,de->sbe", h_one_all, query_key_value_weight, preferred_element_type=jnp.float32
    ).astype(jnp.bfloat16)
    by_latent = jnp.moveaxis(triple, 1, 0).reshape(num_lat, seq_len, 3, local_heads, HEAD_DIM)
    q_lat = by_latent[:, :, 0]
    k_lat = by_latent[:, :, 1]
    v_lat = by_latent[:, :, 2]
    att_lat, log_total = jax.vmap(attend_one)(q_lat, k_lat, v_lat)
    attended = jnp.moveaxis(att_lat, 0, 1).reshape(seq_len, num_lat, local_dim)
    rows = attended
    branch, _ = shrink(
        jnp.einsum(
            "sbh,dh->sbd", rows, output_projection_weight, preferred_element_type=jnp.float32
        )
    )
    middle = block_inputs + gate_one * branch
    normed_two, recip_two = layer_norm(middle)
    h_two = (normed_two * (1.0 + scale_two) + shift_two).astype(jnp.bfloat16)
    h_two_all = spread(h_two)
    hidden = jnp.einsum(
        "sbd,df->sbf", h_two_all, first_dense_weight, preferred_element_type=jnp.float32
    )
    active = jax.nn.gelu(hidden, approximate=True).astype(jnp.bfloat16)
    cotangent = grad_out.astype(jnp.float32)
    grad_mlp = (cotangent * gate_two).astype(jnp.bfloat16)
    grad_mlp_all = spread(grad_mlp)
    grad_fc2 = jnp.einsum(
        "sbd,sbf->df", grad_mlp_all, active, preferred_element_type=jnp.float32
    ).astype(jnp.bfloat16)
    second_dense_weight, grad_fc2 = lax.optimization_barrier((second_dense_weight, grad_fc2))
    grad_fc2 = scatter_rows(grad_fc2).T
    grad_active = jnp.einsum(
        "sbd,df->sbf", grad_mlp_all, second_dense_weight, preferred_element_type=jnp.float32
    )
    gelu_value, gelu_pull = jax.vjp(lambda inner: jax.nn.gelu(inner, approximate=True), hidden)
    grad_hidden = gelu_pull(grad_active)[0].astype(jnp.bfloat16)
    grad_fc1 = jnp.einsum(
        "sbd,sbf->df", h_two_all, grad_hidden, preferred_element_type=jnp.float32
    ).astype(jnp.bfloat16)
    grad_h_two, grad_fc1 = shrink(
        jnp.einsum(
            "sbf,df->sbd", grad_hidden, first_dense_weight, preferred_element_type=jnp.float32
        ),
        grad_fc1,
    )
    grad_fc1 = scatter_rows(grad_fc1)
    grad_shift_two = jnp.sum(grad_h_two, axis=0)
    grad_scale_two = jnp.sum(grad_h_two * normed_two, axis=0)
    grad_middle = cotangent + norm_back(grad_h_two * (1.0 + scale_two), normed_two, recip_two)
    grad_gate_one = jnp.sum(grad_middle * branch, axis=0)
    grad_branch = (grad_middle * gate_one).astype(jnp.bfloat16)
    mlp_terms = jnp.einsum(
        "sbf,df->sbd", active, second_dense_weight, preferred_element_type=jnp.float32
    ).astype(jnp.bfloat16)
    grad_branch_all, mlp_terms = lax.optimization_barrier((spread(grad_branch), mlp_terms))
    mlp_branch, _ = shrink(mlp_terms)
    out_block = (middle + gate_two * mlp_branch).astype(jnp.bfloat16)
    grad_gate_two = jnp.sum(cotangent * mlp_branch, axis=0)
    grad_wout = jnp.einsum(
        "sbd,sbh->dh", grad_branch_all, attended, preferred_element_type=jnp.float32
    )
    grad_att = jnp.einsum(
        "sbd,dh->sbh", grad_branch_all, output_projection_weight, preferred_element_type=jnp.float32
    ).astype(jnp.bfloat16)
    grad_att_lat = jnp.moveaxis(grad_att, 1, 0).reshape(num_lat, seq_len, local_heads, HEAD_DIM)
    grad_triple_lat = jax.vmap(attend_back)(q_lat, k_lat, v_lat, grad_att_lat, log_total)
    grad_triple = jnp.moveaxis(grad_triple_lat, 0, 1).reshape(seq_len, num_lat, 3 * local_dim)
    grad_wqkv = jnp.einsum("sbd,sbe->de", h_one_all, grad_triple, preferred_element_type=jnp.float32)
    grad_attn = jnp.concatenate([grad_wqkv, grad_wout], axis=1).astype(jnp.bfloat16)
    grad_h_one, grad_attn = shrink(
        jnp.einsum(
            "sbe,de->sbd", grad_triple, query_key_value_weight, preferred_element_type=jnp.float32
        ),
        grad_attn,
    )
    grad_attn = scatter_rows(grad_attn)
    grad_shift_one = jnp.sum(grad_h_one, axis=0)
    grad_scale_one = jnp.sum(grad_h_one * normed_one, axis=0)
    grad_input = grad_middle + norm_back(grad_h_one * (1.0 + scale_one), normed_one, recip_one)
    grad_mod_part = jnp.stack(
        [
            grad_shift_one,
            grad_scale_one,
            grad_gate_one,
            grad_shift_two,
            grad_scale_two,
            grad_gate_two,
        ],
        axis=1,
    )
    grad_mod = narrow(grad_mod_part).astype(jnp.bfloat16)
    grad_mod_all = lax.all_gather(grad_mod, "dp", axis=0, tiled=True)
    grad_wmod = jnp.einsum(
        "bd,bke->dke", silu_rows, grad_mod_all, preferred_element_type=jnp.float32
    )
    grad_silu_part = jnp.einsum(
        "bke,dke->bd", grad_mod_all, mod_weight, preferred_element_type=jnp.float32
    )
    grad_silu_part = lax.all_to_all(grad_silu_part, "dp", split_axis=0, concat_axis=1, tiled=True)
    if paired():
        grad_silu = grad_silu_part + lax.ppermute(grad_silu_part, "tensor", SWAP)
    else:
        grad_silu = lax.psum(grad_silu_part, "tensor")
    silu_value, silu_pull = jax.vjp(jax.nn.silu, cond_f)
    grad_condition = silu_pull(grad_silu)[0]
    grad_qkv = grad_attn[:, : 3 * local_dim].reshape(mod_rows, 3, local_dim)
    grad_out_weight = grad_attn[:, 3 * local_dim :].T
    return (
        out_block,
        grad_input,
        grad_condition,
        grad_wmod,
        grad_qkv,
        grad_out_weight,
        grad_fc1,
        grad_fc2,
    )


def solution(mesh):
    return jax.shard_map(
        body,
        mesh=mesh,
        in_specs=(
            P("tensor", "dp", None),
            P("dp", None),
            P("dp", None, "tensor"),
            P("dp", None, "tensor"),
            P("tensor", "dp"),
            P("dp", "tensor"),
            P("tensor", "dp"),
            P("tensor", "dp", None),
        ),
        out_specs=(
            P("tensor", "dp", None),
            P("tensor", "dp", None),
            P("dp", None),
            P("dp", None, "tensor"),
            P("dp", None, "tensor"),
            P("tensor", "dp"),
            P("dp", "tensor"),
            P("tensor", "dp"),
        ),
        check_vma=False,
    )
```

```python
import jax
import jax.numpy as jnp
from jax import lax
from jax.sharding import PartitionSpec as P

HEAD_DIM = 72


eps_norm = 1e-06


def layer_norm(values):
    centred = values - jnp.mean(values, axis=-1, keepdims=True)
    recip = lax.rsqrt(jnp.mean(centred * centred, axis=-1, keepdims=True) + eps_norm)
    return (centred * recip, recip)


def norm_back(grad_norm, normed, recip):
    inner = grad_norm - jnp.mean(grad_norm, axis=-1, keepdims=True)
    return recip * (inner - normed * jnp.mean(grad_norm * normed, axis=-1, keepdims=True))


def attend_one(queries, key_rows, value_rows):
    scores = jnp.einsum(
        "qhe,khe->hqk", queries, key_rows, preferred_element_type=jnp.float32
    ) * HEAD_DIM ** (-0.5)
    peak = jnp.max(scores, axis=-1, keepdims=True)
    raised = jnp.exp(scores - peak)
    total = jnp.sum(raised, axis=-1, keepdims=True)
    attn_probs = (raised / total).astype(jnp.bfloat16)
    attended = jnp.einsum(
        "hqk,khe->qhe", attn_probs, value_rows, preferred_element_type=jnp.float32
    )
    return (attended.astype(jnp.bfloat16), peak + jnp.log(total))


def attend_back(queries, key_rows, value_rows, grad_att, log_total):
    scale = HEAD_DIM ** (-0.5)
    scores = (
        jnp.einsum("qhe,khe->hqk", queries, key_rows, preferred_element_type=jnp.float32) * scale
    )
    attn_probs = jnp.exp(scores - log_total)
    probs_low = attn_probs.astype(jnp.bfloat16)
    grad_probs = jnp.einsum(
        "qhe,khe->hqk", grad_att, value_rows, preferred_element_type=jnp.float32
    )
    centre = jnp.sum(attn_probs * grad_probs, axis=-1, keepdims=True)
    grad_scores = (attn_probs * (grad_probs - centre)).astype(jnp.bfloat16)
    grad_q = (
        jnp.einsum("hqk,khe->qhe", grad_scores, key_rows, preferred_element_type=jnp.float32)
        * scale
    )
    grad_k = (
        jnp.einsum("hqk,qhe->khe", grad_scores, queries, preferred_element_type=jnp.float32) * scale
    )
    grad_v = jnp.einsum("hqk,qhe->khe", probs_low, grad_att, preferred_element_type=jnp.float32)
    return jnp.stack([grad_q, grad_k, grad_v], axis=1).astype(jnp.bfloat16)


SWAP = [(0, 1), (1, 0)]


def paired():
    return lax.axis_size("tensor") == 2


def spread(rows):
    if paired():
        return jnp.concatenate([rows, lax.ppermute(rows, "tensor", SWAP)], axis=0)
    return lax.all_gather(rows, "tensor", axis=0, tiled=True)


def fetch(rows):
    if paired():
        return lax.ppermute(rows, "tensor", SWAP)
    return lax.all_gather(rows, "tensor", axis=0, tiled=True)


def over_all(rows, fetched, change):
    if paired():
        return jnp.concatenate([change(rows), change(fetched)], axis=0)
    return change(fetched)


def shrink(terms, beside=()):
    terms = terms.astype(jnp.bfloat16)
    if paired():
        half = terms.shape[0] // 2
        other = lax.ppermute(terms[half:], "tensor", SWAP)
        other, beside = lax.optimization_barrier((other, beside))
        return terms[:half].astype(jnp.float32) + other.astype(jnp.float32), beside
    total = lax.psum_scatter(terms, "tensor", scatter_dimension=0, tiled=True)
    return total.astype(jnp.float32), beside


def widen(part):
    if paired():
        other = lax.ppermute(part, "tensor", SWAP)
        first = lax.axis_index("tensor") == 0
        return jnp.where(
            first,
            jnp.concatenate([part, other], axis=-1),
            jnp.concatenate([other, part], axis=-1),
        )
    return lax.all_gather(part, "tensor", axis=2, tiled=True)


def narrow(terms):
    if paired():
        half = terms.shape[2] // 2
        first = lax.axis_index("tensor") == 0
        low, high = terms[:, :, :half], terms[:, :, half:]
        other = lax.ppermute(jnp.where(first, high, low), "tensor", SWAP)
        return jnp.where(first, low, high) + other
    return lax.psum_scatter(terms, "tensor", scatter_dimension=2, tiled=True)


def scatter_rows(grad):
    return lax.psum_scatter(grad, "dp", scatter_dimension=0, tiled=True).astype(jnp.float32)


def body(latent_tokens, cond, mod_weight, qkv_weight, out_weight, fc1_weight, fc2_weight, grad_out):
    num_lat = latent_tokens.shape[1]
    local_dim = qkv_weight.shape[2]
    mod_rows = mod_weight.shape[0]
    cond_f = cond.astype(jnp.float32)
    silu_cond = jax.nn.silu(cond_f).astype(jnp.bfloat16)
    silu_rows = lax.all_to_all(silu_cond, "dp", split_axis=1, concat_axis=0, tiled=True)
    mod_terms = jnp.einsum(
        "bd,dke->bke", silu_rows, mod_weight, preferred_element_type=jnp.float32
    )
    mod_terms = mod_terms.reshape(-1, num_lat, 6 * local_dim)
    mod_terms = lax.all_to_all(mod_terms, "dp", split_axis=0, concat_axis=0, tiled=True)
    mod_terms, latent_fetched = lax.optimization_barrier((mod_terms, fetch(latent_tokens)))
    mod_part = jnp.sum(mod_terms, axis=0).reshape(num_lat, 6, local_dim)
    modulation = widen(mod_part)
    query_key_value_weight = lax.all_gather(
        qkv_weight.reshape(mod_rows, -1), "dp", axis=0, tiled=True
    )
    output_projection_weight = lax.all_gather(out_weight.T, "dp", axis=0, tiled=True)
    first_dense_weight = lax.all_gather(fc1_weight, "dp", axis=0, tiled=True)
    second_dense_weight = lax.all_gather(fc2_weight.T, "dp", axis=0, tiled=True)
    local_heads = local_dim // HEAD_DIM
    shift_one, scale_one, gate_one, shift_two, scale_two, gate_two = [
        modulation[None, :, member] for member in range(6)
    ]
    block_inputs = latent_tokens.astype(jnp.float32)
    normed_one, recip_one = layer_norm(block_inputs)
    h_one_all = over_all(
        latent_tokens,
        latent_fetched,
        lambda rows: (
            layer_norm(rows.astype(jnp.float32))[0] * (1.0 + scale_one) + shift_one
        ).astype(jnp.bfloat16),
    )
    seq_len = h_one_all.shape[0]
    triple = jnp.einsum(
        "sbd,de->sbe", h_one_all, query_key_value_weight, preferred_element_type=jnp.float32
    ).astype(jnp.bfloat16)
    by_latent = jnp.moveaxis(triple, 1, 0).reshape(num_lat, seq_len, 3, local_heads, HEAD_DIM)
    q_lat = by_latent[:, :, 0]
    k_lat = by_latent[:, :, 1]
    v_lat = by_latent[:, :, 2]
    att_lat, log_total = jax.vmap(attend_one)(q_lat, k_lat, v_lat)
    attended = jnp.moveaxis(att_lat, 0, 1).reshape(seq_len, num_lat, local_dim)
    attended, grad_out_fetched = lax.optimization_barrier((attended, fetch(grad_out)))
    rows = attended
    branch, _ = shrink(
        jnp.einsum(
            "sbh,dh->sbd", rows, output_projection_weight, preferred_element_type=jnp.float32
        )
    )
    middle = block_inputs + gate_one * branch
    normed_two, recip_two = layer_norm(middle)
    h_two = (normed_two * (1.0 + scale_two) + shift_two).astype(jnp.bfloat16)
    h_two_all = spread(h_two)
    hidden = jnp.einsum(
        "sbd,df->sbf", h_two_all, first_dense_weight, preferred_element_type=jnp.float32
    )
    active = jax.nn.gelu(hidden, approximate=True).astype(jnp.bfloat16)
    cotangent = grad_out.astype(jnp.float32)
    grad_mlp_all = over_all(
        grad_out,
        grad_out_fetched,
        lambda rows: (rows.astype(jnp.float32) * gate_two).astype(jnp.bfloat16),
    )
    grad_fc2 = jnp.einsum(
        "sbd,sbf->df", grad_mlp_all, active, preferred_element_type=jnp.float32
    ).astype(jnp.bfloat16)
    second_dense_weight, grad_fc2 = lax.optimization_barrier((second_dense_weight, grad_fc2))
    grad_fc2 = scatter_rows(grad_fc2).T
    grad_active = jnp.einsum(
        "sbd,df->sbf", grad_mlp_all, second_dense_weight, preferred_element_type=jnp.float32
    )
    gelu_value, gelu_pull = jax.vjp(lambda inner: jax.nn.gelu(inner, approximate=True), hidden)
    grad_hidden = gelu_pull(grad_active)[0].astype(jnp.bfloat16)
    grad_fc1 = jnp.einsum(
        "sbd,sbf->df", h_two_all, grad_hidden, preferred_element_type=jnp.float32
    ).astype(jnp.bfloat16)
    grad_h_two, grad_fc1 = shrink(
        jnp.einsum(
            "sbf,df->sbd", grad_hidden, first_dense_weight, preferred_element_type=jnp.float32
        ),
        grad_fc1,
    )
    grad_fc1 = scatter_rows(grad_fc1)
    grad_shift_two = jnp.sum(grad_h_two, axis=0)
    grad_scale_two = jnp.sum(grad_h_two * normed_two, axis=0)
    grad_middle = cotangent + norm_back(grad_h_two * (1.0 + scale_two), normed_two, recip_two)
    grad_gate_one = jnp.sum(grad_middle * branch, axis=0)
    grad_branch = (grad_middle * gate_one).astype(jnp.bfloat16)
    mlp_terms = jnp.einsum(
        "sbf,df->sbd", active, second_dense_weight, preferred_element_type=jnp.float32
    ).astype(jnp.bfloat16)
    grad_branch_all, mlp_terms = lax.optimization_barrier((spread(grad_branch), mlp_terms))
    grad_wout = jnp.einsum(
        "sbd,sbh->dh", grad_branch_all, attended, preferred_element_type=jnp.float32
    )
    grad_att = jnp.einsum(
        "sbd,dh->sbh", grad_branch_all, output_projection_weight, preferred_element_type=jnp.float32
    ).astype(jnp.bfloat16)
    grad_att_lat = jnp.moveaxis(grad_att, 1, 0).reshape(num_lat, seq_len, local_heads, HEAD_DIM)
    grad_triple_lat = jax.vmap(attend_back)(q_lat, k_lat, v_lat, grad_att_lat, log_total)
    mlp_branch, grad_triple_lat = shrink(mlp_terms, grad_triple_lat)
    out_block = (middle + gate_two * mlp_branch).astype(jnp.bfloat16)
    grad_gate_two = jnp.sum(cotangent * mlp_branch, axis=0)
    grad_triple = jnp.moveaxis(grad_triple_lat, 0, 1).reshape(seq_len, num_lat, 3 * local_dim)
    grad_wqkv = jnp.einsum("sbd,sbe->de", h_one_all, grad_triple, preferred_element_type=jnp.float32)
    grad_attn = jnp.concatenate([grad_wqkv, grad_wout], axis=1).astype(jnp.bfloat16)
    grad_h_one, grad_attn = shrink(
        jnp.einsum(
            "sbe,de->sbd", grad_triple, query_key_value_weight, preferred_element_type=jnp.float32
        ),
        grad_attn,
    )
    grad_attn = scatter_rows(grad_attn)
    grad_shift_one = jnp.sum(grad_h_one, axis=0)
    grad_scale_one = jnp.sum(grad_h_one * normed_one, axis=0)
    grad_input = grad_middle + norm_back(grad_h_one * (1.0 + scale_one), normed_one, recip_one)
    grad_mod_part = jnp.stack(
        [
            grad_shift_one,
            grad_scale_one,
            grad_gate_one,
            grad_shift_two,
            grad_scale_two,
            grad_gate_two,
        ],
        axis=1,
    )
    grad_mod = narrow(grad_mod_part).astype(jnp.bfloat16)
    grad_mod_all = lax.all_gather(grad_mod, "dp", axis=0, tiled=True)
    grad_wmod = jnp.einsum(
        "bd,bke->dke", silu_rows, grad_mod_all, preferred_element_type=jnp.float32
    )
    grad_silu_part = jnp.einsum(
        "bke,dke->bd", grad_mod_all, mod_weight, preferred_element_type=jnp.float32
    )
    grad_silu_part = lax.all_to_all(grad_silu_part, "dp", split_axis=0, concat_axis=1, tiled=True)
    if paired():
        grad_silu = grad_silu_part + lax.ppermute(grad_silu_part, "tensor", SWAP)
    else:
        grad_silu = lax.psum(grad_silu_part, "tensor")
    silu_value, silu_pull = jax.vjp(jax.nn.silu, cond_f)
    grad_condition = silu_pull(grad_silu)[0]
    grad_qkv = grad_attn[:, : 3 * local_dim].reshape(mod_rows, 3, local_dim)
    grad_out_weight = grad_attn[:, 3 * local_dim :].T
    return (
        out_block,
        grad_input,
        grad_condition,
        grad_wmod,
        grad_qkv,
        grad_out_weight,
        grad_fc1,
        grad_fc2,
    )


def solution(mesh):
    return jax.shard_map(
        body,
        mesh=mesh,
        in_specs=(
            P("tensor", "dp", None),
            P("dp", None),
            P("dp", None, "tensor"),
            P("dp", None, "tensor"),
            P("tensor", "dp"),
            P("dp", "tensor"),
            P("tensor", "dp"),
            P("tensor", "dp", None),
        ),
        out_specs=(
            P("tensor", "dp", None),
            P("tensor", "dp", None),
            P("dp", None),
            P("dp", None, "tensor"),
            P("dp", None, "tensor"),
            P("tensor", "dp"),
            P("dp", "tensor"),
            P("tensor", "dp"),
        ),
        check_vma=False,
    )
```
